32 devices in a mesh: row: 4 (over x, core), col: 8 (over z, y).
Axes of the slice: x: 2, y: 2, z: 4, core: 2. Of those that a mesh axis runs over, the one named last changes fastest.
Arguments:
- slab_feat: bfloat16 [8192, 64], P(('row', 'col')), may hold values from -0.8984375 to 0.8984375
- slab_left: bfloat16 [8192, 32], P(('row', 'col')), may hold values from -6 to 6
- points: bfloat16 [16384, 64], P('col'), may hold values from -0.8984375 to 0.8984375
- right_vec: bfloat16 [16384, 32], P('col'), may hold values from -6 to 6
- inv_length: float32 [64], replicated, may hold values from 0.5 to 2
Outputs:
- slab_grad: float32 [8192, 64], P(('row', 'col'))
- point_grad: float32 [16384, 64], P('col')
The draws below stay inside these ranges and needn't reach their ends.
All inputs are finite; a program needn't handle non-finite values.
Results may differ from the reference program's by a relative error of at most 0.0075.
Values may be sent and summed in bfloat16 or wider, within the bound.
A program may use at most 64 MiB of HBM per device.

```python
import math
import jax
import jax.numpy as jnp
from jax import lax

F = 64
RANKS = 32
SLAB = 8192
NPTS = 16384


def level_of(key, dims, cuts, least, largest):
    gain, own = 1.0, jax.random.fold_in(key, 6)
    for position, blocks in cuts:
        steps = jnp.exp(jax.random.uniform(jax.random.fold_in(own, position), (blocks,), jnp.float32, least / len(cuts), largest / len(cuts)))
        gain = gain * jnp.repeat(steps, dims[position] // blocks).reshape([-1 if axis == position else 1 for axis in range(len(dims))])
    return gain


def centred(own_key, dims, spread, bound, split=(), dtype=jnp.bfloat16):
    drawn = spread * jax.random.normal(own_key, dims, jnp.float32)
    if split:
        drawn = drawn * level_of(own_key, dims, split, -0.22, 0.18)
    return jnp.clip(drawn, -bound, bound).astype(dtype)


def setup_inputs(seed: int = 0) -> dict:
    keys = jax.random.split(jax.random.key(seed), 6)
    return {
        "slab_feat": centred(keys[0], (SLAB, F), 0.15, 0.8984375, ((0, 32),)),
        "slab_left": centred(keys[1], (SLAB, RANKS), 1.0, 6.0, ((0, 32),)),
        "points": centred(keys[2], (NPTS, F), 0.15, 0.8984375, ((0, 8),)),
        "right_vec": centred(keys[3], (NPTS, RANKS), 1.0, 6.0, ((0, 8),)),
        "inv_length": jnp.clip(jnp.exp(jax.random.uniform(keys[4], (F,), jnp.float32, math.log(0.5), math.log(2.0))), 0.5, 2.0),
    }


def sweep(xs, left, zs, right, inv_length):
    rows, width = xs.shape
    cols = zs.shape[0]
    ranks = left.shape[1]
    row_block = min(2048, rows)
    col_block = min(256, cols)
    sq_x = lax.optimization_barrier(jnp.sum(jnp.square(xs.astype(jnp.float32)), 1))
    sq_z = lax.optimization_barrier(jnp.sum(jnp.square(zs.astype(jnp.float32)), 1))
    zs_blocks = zs.reshape(cols // col_block, col_block, width)
    right_blocks = right.reshape(cols // col_block, col_block, ranks)
    sqz_blocks = sq_z.reshape(cols // col_block, col_block)
    xs_blocks = xs.reshape(rows // row_block, row_block, width)
    left_blocks = left.reshape(rows // row_block, row_block, ranks)
    sqx_blocks = sq_x.reshape(rows // row_block, row_block)

    def row_step(carry, pieces):
        trans_acc, col_mass = carry
        x_blk, l_blk, sx_blk = pieces

        def col_step(inner, cpieces):
            gz_acc, mass = inner
            z_blk, r_blk, sz_blk = cpieces
            cross = jnp.dot(x_blk, z_blk.T, preferred_element_type=jnp.float32)
            kern = jnp.exp(-0.5 * (sx_blk[:, None] + sz_blk[None, :] - 2.0 * cross))
            weight = jnp.dot(l_blk, r_blk.T, preferred_element_type=jnp.float32)
            prod = weight * kern
            prod_b = prod.astype(jnp.bfloat16)
            gz_acc = gz_acc + jnp.dot(prod_b, z_blk, preferred_element_type=jnp.float32)
            mass = mass + lax.optimization_barrier(jnp.sum(prod, 1))
            trans = jnp.dot(prod_b.T, x_blk, preferred_element_type=jnp.float32)
            return ((gz_acc, mass), (trans, lax.optimization_barrier(jnp.sum(prod, 0))))
        start = (jnp.zeros((row_block, width), jnp.float32), jnp.zeros((row_block,), jnp.float32))
        (gz_acc, mass), (trans, cmass) = lax.scan(col_step, start, (zs_blocks, right_blocks, sqz_blocks))
        trans_acc = trans_acc + trans.reshape(cols, width)
        col_mass = col_mass + cmass.reshape(cols)
        row_term = gz_acc - mass[:, None] * x_blk.astype(jnp.float32)
        return ((trans_acc, col_mass), row_term)
    init = (jnp.zeros((cols, width), jnp.float32), jnp.zeros((cols,), jnp.float32))
    (trans_acc, col_mass), row_terms = lax.scan(row_step, init, (xs_blocks, left_blocks, sqx_blocks))
    row_term = row_terms.reshape(rows, width) * inv_length[None, :]
    col_term = (trans_acc - col_mass[:, None] * zs.astype(jnp.float32)) * inv_length[None, :]
    return (row_term, col_term)

def reference(slab_feat, slab_left, points, right_vec, inv_length):
    ranks = slab_left.shape[1]
    total = points.shape[0]
    coef = jnp.where(jnp.arange(ranks) == 0, 0.5, -0.5 / (ranks - 1)).astype(jnp.float32)
    xs = (slab_feat.astype(jnp.float32) * inv_length[None, :]).astype(jnp.bfloat16)
    zs = (points.astype(jnp.float32) * inv_length[None, :]).astype(jnp.bfloat16)
    left = (slab_left.astype(jnp.float32) * coef[None, :] * (64.0 / math.sqrt(total))).astype(jnp.bfloat16)
    slab_grad, point_grad = sweep(xs, left, zs, right_vec, inv_length)
    return (slab_grad, point_grad)
```

```python
import functools
import math

import jax
import jax.numpy as jnp
from jax import lax
from jax.experimental import pallas as pl
from jax.experimental.pallas import tpu as pltpu
from jax.sharding import PartitionSpec as P

F32 = jnp.float32
BF16 = jnp.bfloat16
MESH = pl.DeviceIdType.MESH
CHUNKS = 2
ONE_X = 64
ONE_Z = 67
LEFT = 96


def split3(v):
    a = v.astype(BF16).astype(F32)
    b = (v - a).astype(BF16).astype(F32)
    return a, b, v - a - b


def packed(scaled, extra, first_sq, first_one):
    rows = scaled.shape[0]
    a, b, c = split3(-0.5 * jnp.sum(scaled * scaled, axis=1, keepdims=True))
    lane = lax.broadcasted_iota(jnp.int32, (rows, 128), 1)
    out = jnp.concatenate([scaled, extra], axis=1)
    out = jnp.where((lane >= first_one) & (lane < first_one + 3), 1.0, out)
    out = jnp.where(lane == first_sq, a, out)
    out = jnp.where(lane == first_sq + 1, b, out)
    return jnp.where(lane == first_sq + 2, c, out)


def kernel(
    n, nrow, total, feat_ref, left_ref, pts_ref, right_ref, inv_ref, slab_ref, point_ref,
    pk, pkt, zp, zpt, rpt, gz, tr, back_out, back_in, a_own, a_in, b_own, b_in,
    g_send, g_recv, r_send, r_recv, a_send, a_recv, b_send, b_recv,
):
    me = lax.axis_index("col")
    row = lax.axis_index("row")
    core = row % 2
    mate = row + 1 - 2 * core
    across = ((row // 2 + 1) % 2) * 2
    rows, width = feat_ref.shape
    ranks = left_ref.shape[1]
    chunks, _, cols = zpt.shape
    half = rows // 2

    def peer(d):
        out = 0
        bit = 1
        while bit < n:
            out = out + (((me // bit) % 2 + (d // bit) % 2) % 2) * bit
            bit *= 2
        return out

    barrier = pltpu.get_barrier_semaphore()
    for d in range(1, n):
        pl.semaphore_signal(barrier, inc=1, device_id={"col": peer(d)}, device_id_type=MESH)
    for r in (mate, across, across + 1):
        pl.semaphore_signal(barrier, inc=1, device_id={"row": r}, device_id_type=MESH)

    inv = inv_ref[...]
    xs = (feat_ref[...].astype(F32) * inv).astype(BF16).astype(F32)
    rank = lax.broadcasted_iota(jnp.int32, (rows, ranks), 1)
    coef = jnp.where(rank == 0, jnp.float32(0.5), jnp.float32(-0.5 / (ranks - 1)))
    left = left_ref[...].astype(F32) * coef * (64.0 / math.sqrt(total))
    extra = jnp.concatenate([jnp.zeros((rows, LEFT - width), F32), left], axis=1)
    pk[0] = packed(xs, extra, ONE_Z, ONE_X).astype(BF16)
    pl.semaphore_wait(barrier, n + 2)

    def gather(d):
        return pltpu.make_async_remote_copy(
            src_ref=pk.at[0], dst_ref=pk.at[d], send_sem=g_send.at[d], recv_sem=g_recv.at[d],
            device_id={"col": peer(d)}, device_id_type=MESH,
        )

    def giveback(d):
        return pltpu.make_async_remote_copy(
            src_ref=back_out.at[d], dst_ref=back_in.at[d], send_sem=r_send.at[d],
            recv_sem=r_recv.at[d], device_id={"col": peer(d)}, device_id_type=MESH,
        )

    def stage_a(h):
        return pltpu.make_async_remote_copy(
            src_ref=a_own.at[h], dst_ref=a_in.at[h], send_sem=a_send.at[h],
            recv_sem=a_recv.at[h], device_id={"row": mate}, device_id_type=MESH,
        )

    def stage_b(h, side, slot):
        return pltpu.make_async_remote_copy(
            src_ref=b_own.at[h, slot], dst_ref=b_in.at[h, slot], send_sem=b_send.at[h, side],
            recv_sem=b_recv.at[h, slot], device_id={"row": across + side}, device_id_type=MESH,
        )

    for d in range(1, n):
        gather(d).start()

    for h in range(chunks):
        part = pl.ds(h * cols, cols)
        zs = (pts_ref[part, :].astype(F32) * inv).astype(BF16).astype(F32)
        zpk = packed(zs, jnp.zeros((cols, 128 - width), F32), ONE_X, ONE_Z)
        zp[h] = zpk.astype(BF16)
        zpt[h] = zpk.T.astype(BF16)
        rp = jnp.concatenate(
            [jnp.zeros((cols, LEFT), F32), right_ref[part, :].astype(F32)], axis=1
        )
        rpt[h] = rp.T.astype(BF16)

    def send_a(h):
        zt = zpt[h, :width, :].astype(F32)
        term = tr[:width, :] - tr[ONE_X:ONE_X + 1, :] * zt
        a_own[h] = term.astype(BF16)
        stage_a(h).start()

    def send_b(h):
        stage_a(h).wait()
        s = (a_own[h].astype(F32) + a_in[h].astype(F32)).astype(BF16)
        b_own[h, 0] = s[:, : cols // 2]
        b_own[h, 1] = s[:, cols // 2:]
        for side in range(2):
            stage_b(h, side, core).start()

    def finish(h):
        for side in range(2):
            stage_b(h, side, core).wait_send()
        for slot in range(2):
            stage_b(h, 0, slot).wait_recv()
        for slot in range(2):
            tot = b_own[h, slot].astype(F32) + b_in[h, slot].astype(F32)
            w = cols // 2
            point_ref[pl.ds(h * cols + slot * w, w), :] = tot.T * inv

    def step(i, carry):
        h = i // n
        k = i % n
        last = h == chunks - 1
        d = jnp.where(last, n - 1 - k, k)

        @pl.when((h == 0) & (d > 0))
        def _():
            gather(d).wait()

        @pl.when(h == 0)
        def _():
            pkt[d] = pk[d].astype(F32).T[: pkt.shape[1], :].astype(BF16)

        block = pk[d]
        arg = jnp.dot(block, zpt[h], preferred_element_type=F32)
        weight = jnp.dot(block, rpt[h], preferred_element_type=F32)
        prod = (weight * jnp.exp(arg)).astype(BF16)
        g = jnp.dot(prod, zp[h], preferred_element_type=F32)
        t = jnp.dot(pkt[d], prod, preferred_element_type=F32)
        gz[d] = jnp.where(h == 0, 0.0, gz[d]) + g
        tr[...] = jnp.where(k == 0, 0.0, tr[...]) + t

        @pl.when(last)
        def _():
            acc = gz[d]
            term = acc[:, :width] - acc[:, ONE_Z:ONE_Z + 1] * pk[d][:, :width].astype(F32)
            both = jnp.concatenate([term[:half], term[half:]], axis=1)

            @pl.when(d > 0)
            def _():
                back_out[d] = both.astype(BF16)
                giveback(d).start()

            @pl.when(d == 0)
            def _():
                gz[0] = jnp.concatenate([both, both], axis=0)

        @pl.when(k == n - 1)
        def _():
            send_a(h)

        @pl.when((h > 0) & (k == 1))
        def _():
            send_b(h - 1)

        @pl.when((h > 0) & (k == n - 2))
        def _():
            finish(h - 1)

        return carry

    lax.fori_loop(0, chunks * n, step, 0)

    for d in range(1, n):
        giveback(d).wait()

    def add(d, acc):
        return acc + back_in[d].astype(F32)

    acc = lax.fori_loop(1, n, add, gz[0, :half, :])
    slab_ref[:half, :] = acc[:, :width] * inv
    slab_ref[half:, :] = acc[:, width:] * inv
    send_b(chunks - 1)
    finish(chunks - 1)


def local(n, nrow, slab_feat, slab_left, points, right_vec, inv_length):
    rows, width = slab_feat.shape
    npts = points.shape[0]
    cols = npts // CHUNKS
    vm = pl.BlockSpec(memory_space=pltpu.VMEM)
    dma = pltpu.SemaphoreType.DMA
    flops = 2 * n * rows * npts * 4 * 128
    return pl.pallas_call(
        functools.partial(kernel, n, nrow, npts * n),
        out_shape=(
            jax.ShapeDtypeStruct((rows, width), F32),
            jax.ShapeDtypeStruct((npts, width), F32),
        ),
        in_specs=[vm] * 5,
        out_specs=(vm, vm),
        scratch_shapes=[
            pltpu.VMEM((n, rows, 128), BF16),
            pltpu.VMEM((n, 80, rows), BF16),
            pltpu.VMEM((CHUNKS, cols, 128), BF16),
            pltpu.VMEM((CHUNKS, 128, cols), BF16),
            pltpu.VMEM((CHUNKS, 128, cols), BF16),
            pltpu.VMEM((n, rows, 128), F32),
            pltpu.VMEM((80, cols), F32),
            pltpu.VMEM((n, rows // 2, 128), BF16),
            pltpu.VMEM((n, rows // 2, 128), BF16),
            pltpu.VMEM((CHUNKS, width, cols), BF16),
            pltpu.VMEM((CHUNKS, width, cols), BF16),
            pltpu.VMEM((CHUNKS, 2, width, cols // 2), BF16),
            pltpu.VMEM((CHUNKS, 2, width, cols // 2), BF16),
            dma((n,)),
            dma((n,)),
            dma((n,)),
            dma((n,)),
            dma((CHUNKS,)),
            dma((CHUNKS,)),
            dma((CHUNKS, 2)),
            dma((CHUNKS, 2)),
        ],
        compiler_params=pltpu.CompilerParams(
            collective_id=0, has_side_effects=True, vmem_limit_bytes=48 * 1024 * 1024
        ),
        cost_estimate=pl.CostEstimate(
            flops=flops, bytes_accessed=4 * 1024 * 1024, transcendentals=n * rows * npts
        ),
    )(slab_feat, slab_left, points, right_vec, inv_length.reshape(1, width))


def solution(mesh):
    placed = (P(("row", "col"), None), P(("row", "col"), None), P("col", None), P("col", None), P())
    return jax.shard_map(
        functools.partial(local, mesh.shape["col"], mesh.shape["row"]),
        mesh=mesh,
        in_specs=placed,
        out_specs=(P(("row", "col"), None), P("col", None)),
        check_vma=False,
    )
```

```python
import functools
import math

import jax
import jax.numpy as jnp
from jax import lax
from jax.experimental import pallas as pl
from jax.experimental.pallas import tpu as pltpu
from jax.sharding import PartitionSpec as P

F32 = jnp.float32
BF16 = jnp.bfloat16
MESH = pl.DeviceIdType.MESH
CHUNKS = 2
ONE_X = 64
ONE_Z = 67
LEFT = 80


def split3(v):
    a = v.astype(BF16).astype(F32)
    b = (v - a).astype(BF16).astype(F32)
    return a, b, v - a - b


def tail_rows(scaled, first_sq, first_one):
    a, b, c = split3(-0.5 * jnp.sum(scaled * scaled, axis=0, keepdims=True))
    line = lax.broadcasted_iota(jnp.int32, (16, scaled.shape[1]), 0) + 64
    out = jnp.where((line >= first_one) & (line < first_one + 3), 1.0, 0.0)
    out = jnp.where(line == first_sq, a, out)
    out = jnp.where(line == first_sq + 1, b, out)
    return jnp.where(line == first_sq + 2, c, out)


def kernel(
    n, total, feat_hbm, left_hbm, pts_hbm, right_hbm, inv_hbm, slab_ref, point_ref,
    feat_ref, left_ref, pts_ref, right_ref, inv_ref,
    gin, pk, pkt, zp, zpt, rpt, gz, tr, back_out, back_in, a_own, a_in, b_own, b_in,
    l_sem, g_send, g_recv, f_send, r_send, r_recv, a_send, a_recv, b_send, b_recv,
):
    me = lax.axis_index("col")
    row = lax.axis_index("row")
    core = row % 2
    mate = row + 1 - 2 * core
    across = ((row // 2 + 1) % 2) * 2
    width, rows = feat_ref.shape
    ranks = left_ref.shape[0]
    chunks, _, cols = zpt.shape

    loads = [
        pltpu.make_async_copy(src, dst, l_sem.at[i])
        for i, (src, dst) in enumerate((
            (inv_hbm, inv_ref), (feat_hbm, feat_ref), (left_hbm, left_ref),
            (pts_hbm, pts_ref), (right_hbm, right_ref),
        ))
    ]
    for load in loads:
        load.start()

    def peer(d):
        out = 0
        bit = 1
        while bit < n:
            out = out + (((me // bit) % 2 + (d // bit) % 2) % 2) * bit
            bit *= 2
        return out

    barrier = pltpu.get_barrier_semaphore()
    for d in range(1, n):
        pl.semaphore_signal(barrier, inc=1, device_id={"col": peer(d)}, device_id_type=MESH)
    for r in (mate, across, across + 1):
        pl.semaphore_signal(barrier, inc=1, device_id={"row": r}, device_id_type=MESH)

    loads[0].wait()
    eye = lax.broadcasted_iota(jnp.int32, (width, width), 0) == lax.broadcasted_iota(
        jnp.int32, (width, width), 1
    )
    inv = jnp.sum(jnp.where(eye, inv_ref[...], 0.0), axis=1, keepdims=True)
    loads[1].wait()
    loads[2].wait()
    gin[0, :width, :] = (feat_ref[...].astype(F32) * inv).astype(BF16)
    rank = lax.broadcasted_iota(jnp.int32, (ranks, rows), 0)
    coef = jnp.where(rank == 0, jnp.float32(0.5), jnp.float32(-0.5 / (ranks - 1)))
    gin[0, width:, :] = (left_ref[...].astype(F32) * coef * (64.0 / math.sqrt(total))).astype(BF16)
    pl.semaphore_wait(barrier, n + 2)

    def gather(d):
        return pltpu.make_async_remote_copy(
            src_ref=gin.at[0], dst_ref=gin.at[d], send_sem=g_send.at[d], recv_sem=g_recv.at[d],
            device_id={"col": peer(d)}, device_id_type=MESH,
        )

    def forward(d):
        return pltpu.make_async_remote_copy(
            src_ref=gin.at[d], dst_ref=gin.at[d + 1], send_sem=f_send.at[d],
            recv_sem=g_recv.at[d + 1], device_id={"col": peer(1)}, device_id_type=MESH,
        )

    def giveback(d):
        return pltpu.make_async_remote_copy(
            src_ref=back_out.at[d], dst_ref=back_in.at[d], send_sem=r_send.at[d],
            recv_sem=r_recv.at[d], device_id={"col": peer(d)}, device_id_type=MESH,
        )

    def stage_a(h):
        return pltpu.make_async_remote_copy(
            src_ref=a_own.at[h], dst_ref=a_in.at[h], send_sem=a_send.at[h],
            recv_sem=a_recv.at[h], device_id={"row": mate}, device_id_type=MESH,
        )

    def stage_b(h, side, slot):
        return pltpu.make_async_remote_copy(
            src_ref=b_own.at[h, slot], dst_ref=b_in.at[h, slot], send_sem=b_send.at[h, side],
            recv_sem=b_recv.at[h, slot], device_id={"row": across + side}, device_id_type=MESH,
        )

    for d in range(2, n, 2):
        gather(d).start()
    gather(1).start()

    loads[3].wait()
    loads[4].wait()
    for h in range(chunks):
        part = pl.ds(h * cols, cols)
        zs = (pts_ref[:, part].astype(F32) * inv).astype(BF16).astype(F32)
        zt = jnp.concatenate(
            [zs, tail_rows(zs, ONE_X, ONE_Z), jnp.zeros((128 - LEFT, cols), F32)], axis=0
        )
        zpt[h] = zt.astype(BF16)
        zp[h] = zt.T.astype(BF16)
        rpt[h] = jnp.concatenate(
            [
                jnp.zeros((LEFT, cols), BF16),
                right_ref[:, part],
                jnp.zeros((128 - LEFT - ranks, cols), BF16),
            ],
            axis=0,
        )

    def send_a(h):
        zt = zpt[h, :width, :].astype(F32)
        term = tr[:width, :] - tr[ONE_X:ONE_X + 1, :] * zt
        a_own[h] = term.astype(BF16)
        stage_a(h).start()

    def send_b(h):
        stage_a(h).wait()
        s = (a_own[h].astype(F32) + a_in[h].astype(F32)).astype(BF16)
        b_own[h, 0] = s[:, : cols // 2]
        b_own[h, 1] = s[:, cols // 2:]
        for side in range(2):
            stage_b(h, side, core).start()

    def finish(h):
        for side in range(2):
            stage_b(h, side, core).wait_send()
        for slot in range(2):
            stage_b(h, 0, slot).wait_recv()
        w = cols // 2
        for slot in range(2):
            tot = b_own[h, slot].astype(F32) + b_in[h, slot].astype(F32)
            point_ref[:, pl.ds(pl.multiple_of(h * cols + slot * w, w), w)] = tot * inv

    def step(i, carry):
        h = i // n
        k = i % n
        last = h == chunks - 1
        even = k <= n // 2
        near = jnp.where(k < 2, k, jnp.where(even, 2 * k - 2, 2 * k - n + 1))
        d = jnp.where(last, n - 1 - k, near)

        @pl.when((h == 0) & (k > 0))
        def _():
            gather(d).wait_recv()

        @pl.when((h == 0) & (k > 1) & even)
        def _():
            forward(d).start()

        @pl.when(h == 0)
        def _():
            x = gin[d].astype(F32)
            xs = x[:width]
            both = jnp.concatenate(
                [
                    xs, tail_rows(xs, ONE_Z, ONE_X), x[width:],
                    jnp.zeros((128 - LEFT - ranks, rows), F32),
                ],
                axis=0,
            )
            pkt[d] = both[:LEFT].astype(BF16)
            pk[d] = both.T.astype(BF16)

        block = pk[d]
        arg = jnp.dot(block, zpt[h], preferred_element_type=F32)
        weight = jnp.dot(block, rpt[h], preferred_element_type=F32)
        prod = (weight * jnp.exp(arg)).astype(BF16)
        g = jnp.dot(prod, zp[h], preferred_element_type=F32)
        t = jnp.dot(pkt[d], prod, preferred_element_type=F32)
        gz[d] = jnp.where(h == 0, 0.0, gz[d]) + g
        tr[...] = jnp.where(k == 0, 0.0, tr[...]) + t

        @pl.when(last)
        def _():
            acc = gz[d].T
            term = acc[:width] - acc[ONE_Z:ONE_Z + 1] * pkt[d][:width].astype(F32)

            @pl.when(d > 0)
            def _():
                back_out[d] = term.astype(BF16)
                giveback(d).start()

            @pl.when(d == 0)
            def _():
                slab_ref[...] = term

        @pl.when(k == n - 1)
        def _():
            send_a(h)

        @pl.when((h > 0) & (k == 1))
        def _():
            send_b(h - 1)

        @pl.when((h > 0) & (k == n - 2))
        def _():
            finish(h - 1)

        return carry

    lax.fori_loop(0, chunks * n, step, 0)

    gather(1).wait_send()
    for d in range(2, n, 2):
        gather(d).wait_send()
        forward(d).wait_send()
    for d in range(1, n):
        giveback(d).wait()

    def add(d, acc):
        return acc + back_in[d].astype(F32)

    acc = lax.fori_loop(1, n, add, slab_ref[...])
    slab_ref[...] = acc * inv
    send_b(chunks - 1)
    finish(chunks - 1)


def local(n, slab_feat, slab_left, points, right_vec, inv_length):
    rows, width = slab_feat.shape
    ranks = slab_left.shape[1]
    npts = points.shape[0]
    cols = npts // CHUNKS
    vm = pl.BlockSpec(memory_space=pltpu.VMEM)
    hbm = pl.BlockSpec(memory_space=pl.ANY)
    dma = pltpu.SemaphoreType.DMA
    flops = 2 * n * rows * npts * 4 * 128
    slab, point = pl.pallas_call(
        functools.partial(kernel, n, npts * n),
        out_shape=(
            jax.ShapeDtypeStruct((width, rows), F32),
            jax.ShapeDtypeStruct((width, npts), F32),
        ),
        in_specs=[hbm] * 5,
        out_specs=(vm, vm),
        scratch_shapes=[
            pltpu.VMEM((width, rows), BF16),
            pltpu.VMEM((ranks, rows), BF16),
            pltpu.VMEM((width, npts), BF16),
            pltpu.VMEM((ranks, npts), BF16),
            pltpu.VMEM((1, width), F32),
            pltpu.VMEM((n, width + ranks, rows), BF16),
            pltpu.VMEM((n, rows, 128), BF16),
            pltpu.VMEM((n, LEFT, rows), BF16),
            pltpu.VMEM((CHUNKS, cols, 128), BF16),
            pltpu.VMEM((CHUNKS, 128, cols), BF16),
            pltpu.VMEM((CHUNKS, 128, cols), BF16),
            pltpu.VMEM((n, rows, 128), F32),
            pltpu.VMEM((LEFT, cols), F32),
            pltpu.VMEM((n, width, rows), BF16),
            pltpu.VMEM((n, width, rows), BF16),
            pltpu.VMEM((CHUNKS, width, cols), BF16),
            pltpu.VMEM((CHUNKS, width, cols), BF16),
            pltpu.VMEM((CHUNKS, 2, width, cols // 2), BF16),
            pltpu.VMEM((CHUNKS, 2, width, cols // 2), BF16),
            dma((5,)),
            dma((n,)),
            dma((n,)),
            dma((n,)),
            dma((n,)),
            dma((n,)),
            dma((CHUNKS,)),
            dma((CHUNKS,)),
            dma((CHUNKS, 2)),
            dma((CHUNKS, 2)),
        ],
        compiler_params=pltpu.CompilerParams(
            collective_id=0, has_side_effects=True, vmem_limit_bytes=48 * 1024 * 1024
        ),
        cost_estimate=pl.CostEstimate(
            flops=flops, bytes_accessed=4 * 1024 * 1024, transcendentals=n * rows * npts
        ),
    )(slab_feat.T, slab_left.T, points.T, right_vec.T, inv_length.reshape(1, width))
    return slab.T, point.T


def solution(mesh):
    placed = (P(("row", "col"), None), P(("row", "col"), None), P("col", None), P("col", None), P())
    return jax.shard_map(
        functools.partial(local, mesh.shape["col"]),
        mesh=mesh,
        in_specs=placed,
        out_specs=(P(("row", "col"), None), P("col", None)),
        check_vma=False,
    )
```

```python
import functools
import math

import jax
import jax.numpy as jnp
from jax import lax
from jax.experimental import pallas as pl
from jax.experimental.pallas import tpu as pltpu
from jax.sharding import PartitionSpec as P

F32 = jnp.float32
BF16 = jnp.bfloat16
MESH = pl.DeviceIdType.MESH
CHUNKS = 2
ONE_X = 64
ONE_Z = 67
LEFT = 80


def split3(v):
    a = v.astype(BF16).astype(F32)
    b = (v - a).astype(BF16).astype(F32)
    return a, b, v - a - b


def tail_rows(scaled, first_sq, first_one):
    a, b, c = split3(-0.5 * jnp.sum(scaled * scaled, axis=0, keepdims=True))
    line = lax.broadcasted_iota(jnp.int32, (16, scaled.shape[1]), 0) + 64
    out = jnp.where((line >= first_one) & (line < first_one + 3), 1.0, 0.0)
    out = jnp.where(line == first_sq, a, out)
    out = jnp.where(line == first_sq + 1, b, out)
    return jnp.where(line == first_sq + 2, c, out)


def kernel(
    n, total, feat_hbm, left_hbm, pts_hbm, right_hbm, inv_hbm, slab_hbm, point_hbm,
    feat_ref, left_ref, pts_ref, right_ref, inv_ref, slab_ref, point_ref,
    gin, pk, pkt, zp, zpt, rpt, gz, tr, back_out, back_in, a_own, a_in, b_own, b_in,
    l_sem, o_sem, g_send, g_recv, f_send, r_send, r_recv, a_send, a_recv, b_send, b_recv,
):
    me = lax.axis_index("col")
    row = lax.axis_index("row")
    core = row % 2
    mate = row + 1 - 2 * core
    across = ((row // 2 + 1) % 2) * 2
    width, rows = feat_ref.shape
    ranks = left_ref.shape[0]
    chunks, _, cols = zpt.shape

    loads = [
        pltpu.make_async_copy(src, dst, l_sem.at[i])
        for i, (src, dst) in enumerate((
            (inv_hbm, inv_ref), (feat_hbm, feat_ref), (left_hbm, left_ref),
            (pts_hbm, pts_ref), (right_hbm, right_ref),
        ))
    ]
    for load in loads:
        load.start()

    def peer(d):
        out = 0
        bit = 1
        while bit < n:
            out = out + (((me // bit) % 2 + (d // bit) % 2) % 2) * bit
            bit *= 2
        return out

    barrier = pltpu.get_barrier_semaphore()
    for d in range(1, n):
        pl.semaphore_signal(barrier, inc=1, device_id={"col": peer(d)}, device_id_type=MESH)
    for r in (mate, across, across + 1):
        pl.semaphore_signal(barrier, inc=1, device_id={"row": r}, device_id_type=MESH)

    loads[0].wait()
    eye = lax.broadcasted_iota(jnp.int32, (width, width), 0) == lax.broadcasted_iota(
        jnp.int32, (width, width), 1
    )
    inv = jnp.sum(jnp.where(eye, inv_ref[...], 0.0), axis=1, keepdims=True)
    loads[1].wait()
    loads[2].wait()
    gin[0, :width, :] = (feat_ref[...].astype(F32) * inv).astype(BF16)
    rank = lax.broadcasted_iota(jnp.int32, (ranks, rows), 0)
    coef = jnp.where(rank == 0, jnp.float32(0.5), jnp.float32(-0.5 / (ranks - 1)))
    gin[0, width:, :] = (left_ref[...].astype(F32) * coef * (64.0 / math.sqrt(total))).astype(BF16)
    pl.semaphore_wait(barrier, n + 2)

    def gather(d):
        return pltpu.make_async_remote_copy(
            src_ref=gin.at[0], dst_ref=gin.at[d], send_sem=g_send.at[d], recv_sem=g_recv.at[d],
            device_id={"col": peer(d)}, device_id_type=MESH,
        )

    def forward(d):
        return pltpu.make_async_remote_copy(
            src_ref=gin.at[d], dst_ref=gin.at[d + 1], send_sem=f_send.at[d],
            recv_sem=g_recv.at[d + 1], device_id={"col": peer(1)}, device_id_type=MESH,
        )

    def giveback(d):
        return pltpu.make_async_remote_copy(
            src_ref=back_out.at[d], dst_ref=back_in.at[d], send_sem=r_send.at[d],
            recv_sem=r_recv.at[d], device_id={"col": peer(d)}, device_id_type=MESH,
        )

    def stage_a(h):
        return pltpu.make_async_remote_copy(
            src_ref=a_own.at[h], dst_ref=a_in.at[h], send_sem=a_send.at[h],
            recv_sem=a_recv.at[h], device_id={"row": mate}, device_id_type=MESH,
        )

    def stage_b(h, side, slot):
        return pltpu.make_async_remote_copy(
            src_ref=b_own.at[h, slot], dst_ref=b_in.at[h, slot], send_sem=b_send.at[h, side],
            recv_sem=b_recv.at[h, slot], device_id={"row": across + side}, device_id_type=MESH,
        )

    for d in range(2, n, 2):
        gather(d).start()
    gather(1).start()

    loads[3].wait()
    loads[4].wait()
    for h in range(chunks):
        part = pl.ds(h * cols, cols)
        zs = (pts_ref[:, part].astype(F32) * inv).astype(BF16).astype(F32)
        zt = jnp.concatenate(
            [zs, tail_rows(zs, ONE_X, ONE_Z), jnp.zeros((128 - LEFT, cols), F32)], axis=0
        )
        zpt[h] = zt.astype(BF16)
        zp[h] = zt.T.astype(BF16)
        rpt[h] = jnp.concatenate(
            [
                jnp.zeros((LEFT, cols), BF16),
                right_ref[:, part],
                jnp.zeros((128 - LEFT - ranks, cols), BF16),
            ],
            axis=0,
        )

    def store(h):
        part = pl.ds(pl.multiple_of(h * cols, cols), cols)
        return pltpu.make_async_copy(point_ref.at[h], point_hbm.at[:, part], o_sem.at[h])

    def send_a(h):
        zt = zpt[h, :width, :].astype(F32)
        term = tr[h, :width, :] - tr[h, ONE_X:ONE_X + 1, :] * zt
        a_own[h] = term.astype(BF16)
        stage_a(h).start()

    def send_b(h):
        stage_a(h).wait()
        s = (a_own[h].astype(F32) + a_in[h].astype(F32)).astype(BF16)
        b_own[h, 0] = s[:, : cols // 2]
        b_own[h, 1] = s[:, cols // 2:]
        for side in range(2):
            stage_b(h, side, core).start()

    def finish(h):
        for side in range(2):
            stage_b(h, side, core).wait_send()
        for slot in range(2):
            stage_b(h, 0, slot).wait_recv()
        tot = b_own[h].astype(F32) + b_in[h].astype(F32)
        point_ref[h] = jnp.concatenate([tot[0], tot[1]], axis=1) * inv
        store(h).start()

    def step(i, carry):
        early = i < 4
        late = i >= n + 2
        h = jnp.where(early, i % 2, jnp.where(late, 1, 0))
        k = i - 2
        even = k <= n // 2
        near = jnp.where(even, 2 * k - 2, 2 * k - n + 1)
        d = jnp.where(early, i // 2, jnp.where(late, 2 * n + 1 - i, near))
        last = h == 1

        @pl.when((h == 0) & (d > 0))
        def _():
            gather(d).wait_recv()

        @pl.when((h == 0) & (d > 1) & even)
        def _():
            forward(d).start()

        @pl.when(h == 0)
        def _():
            x = gin[d].astype(F32)
            xs = x[:width]
            both = jnp.concatenate(
                [
                    xs, tail_rows(xs, ONE_Z, ONE_X), x[width:],
                    jnp.zeros((128 - LEFT - ranks, rows), F32),
                ],
                axis=0,
            )
            pkt[d] = both[:LEFT].astype(BF16)
            pk[d] = both.T.astype(BF16)

        block = pk[d]
        arg = jnp.dot(block, zpt[h], preferred_element_type=F32)
        weight = jnp.dot(block, rpt[h], preferred_element_type=F32)
        prod = (weight * jnp.exp(arg)).astype(BF16)
        g = jnp.dot(prod, zp[h], preferred_element_type=F32)
        t = jnp.dot(pkt[d], prod, preferred_element_type=F32)
        gz[d] = jnp.where(h == 0, 0.0, gz[d]) + g
        tr[h] = jnp.where(d == 0, 0.0, tr[h]) + t

        @pl.when(last)
        def _():
            acc = gz[d].T
            term = acc[:width] - acc[ONE_Z:ONE_Z + 1] * pkt[d][:width].astype(F32)

            @pl.when(d > 0)
            def _():
                back_out[d] = term.astype(BF16)
                giveback(d).start()

            @pl.when(d == 0)
            def _():
                slab_ref[...] = term

        @pl.when(i == n + 1)
        def _():
            send_a(0)

        @pl.when(i == n + 3)
        def _():
            send_b(0)

        @pl.when(i == 2 * n - 1)
        def _():
            send_a(1)
            finish(0)

        return carry

    lax.fori_loop(0, 2 * n, step, 0)

    gather(1).wait_send()
    for d in range(2, n, 2):
        gather(d).wait_send()
        forward(d).wait_send()
    send_b(1)
    for d in range(1, n):
        giveback(d).wait()

    def add(d, acc):
        return acc + back_in[d].astype(F32)

    slab_ref[...] = lax.fori_loop(1, n, add, slab_ref[...]) * inv
    slab_store = pltpu.make_async_copy(slab_ref, slab_hbm, o_sem.at[chunks])
    slab_store.start()
    finish(1)
    slab_store.wait()
    store(0).wait()
    store(1).wait()


def local(n, slab_feat, slab_left, points, right_vec, inv_length):
    rows, width = slab_feat.shape
    ranks = slab_left.shape[1]
    npts = points.shape[0]
    cols = npts // CHUNKS
    hbm = pl.BlockSpec(memory_space=pl.ANY)
    dma = pltpu.SemaphoreType.DMA
    flops = 2 * n * rows * npts * 4 * 128
    slab, point = pl.pallas_call(
        functools.partial(kernel, n, npts * n),
        out_shape=(
            jax.ShapeDtypeStruct((width, rows), F32),
            jax.ShapeDtypeStruct((width, npts), F32),
        ),
        in_specs=[hbm] * 5,
        out_specs=(hbm, hbm),
        scratch_shapes=[
            pltpu.VMEM((width, rows), BF16),
            pltpu.VMEM((ranks, rows), BF16),
            pltpu.VMEM((width, npts), BF16),
            pltpu.VMEM((ranks, npts), BF16),
            pltpu.VMEM((1, width), F32),
            pltpu.VMEM((width, rows), F32),
            pltpu.VMEM((CHUNKS, width, cols), F32),
            pltpu.VMEM((n, width + ranks, rows), BF16),
            pltpu.VMEM((n, rows, 128), BF16),
            pltpu.VMEM((n, LEFT, rows), BF16),
            pltpu.VMEM((CHUNKS, cols, 128), BF16),
            pltpu.VMEM((CHUNKS, 128, cols), BF16),
            pltpu.VMEM((CHUNKS, 128, cols), BF16),
            pltpu.VMEM((n, rows, 128), F32),
            pltpu.VMEM((CHUNKS, LEFT, cols), F32),
            pltpu.VMEM((n, width, rows), BF16),
            pltpu.VMEM((n, width, rows), BF16),
            pltpu.VMEM((CHUNKS, width, cols), BF16),
            pltpu.VMEM((CHUNKS, width, cols), BF16),
            pltpu.VMEM((CHUNKS, 2, width, cols // 2), BF16),
            pltpu.VMEM((CHUNKS, 2, width, cols // 2), BF16),
            dma((5,)),
            dma((CHUNKS + 1,)),
            dma((n,)),
            dma((n,)),
            dma((n,)),
            dma((n,)),
            dma((n,)),
            dma((CHUNKS,)),
            dma((CHUNKS,)),
            dma((CHUNKS, 2)),
            dma((CHUNKS, 2)),
        ],
        compiler_params=pltpu.CompilerParams(
            collective_id=0, has_side_effects=True, vmem_limit_bytes=125 * 512 * 1024
        ),
        cost_estimate=pl.CostEstimate(
            flops=flops, bytes_accessed=4 * 1024 * 1024, transcendentals=n * rows * npts
        ),
    )(slab_feat.T, slab_left.T, points.T, right_vec.T, inv_length.reshape(1, width))
    return slab.T, point.T


def solution(mesh):
    placed = (P(("row", "col"), None), P(("row", "col"), None), P("col", None), P("col", None), P())
    return jax.shard_map(
        functools.partial(local, mesh.shape["col"]),
        mesh=mesh,
        in_specs=placed,
        out_specs=(P(("row", "col"), None), P("col", None)),
        check_vma=False,
    )
```

```python
import functools
import math

import jax
import jax.numpy as jnp
from jax import lax
from jax.experimental import pallas as pl
from jax.experimental.pallas import tpu as pltpu
from jax.sharding import PartitionSpec as P

F32 = jnp.float32
BF16 = jnp.bfloat16
MESH = pl.DeviceIdType.MESH
CHUNKS = 2
ONE_X = 64
ONE_Z = 67
LEFT = 80


def split3(v):
    a = v.astype(BF16).astype(F32)
    b = (v - a).astype(BF16).astype(F32)
    return a, b, v - a - b


def tail_rows(scaled, first_sq, first_one):
    a, b, c = split3(-0.5 * jnp.sum(scaled * scaled, axis=0, keepdims=True))
    line = lax.broadcasted_iota(jnp.int32, (16, scaled.shape[1]), 0) + 64
    out = jnp.where((line >= first_one) & (line < first_one + 3), 1.0, 0.0)
    out = jnp.where(line == first_sq, a, out)
    out = jnp.where(line == first_sq + 1, b, out)
    return jnp.where(line == first_sq + 2, c, out)


def kernel(
    n, total, feat_hbm, left_hbm, pts_hbm, right_hbm, inv_hbm, slab_ref, point_ref,
    feat_ref, left_ref, pts_ref, right_ref, inv_ref,
    gin, pk, pkt, zp, zpt, rpt, gz, tr, back_out, back_in, a_own, a_in, b_own, b_in,
    l_sem, g_send, g_recv, f_send, r_send, r_recv, a_send, a_recv, b_send, b_recv,
):
    me = lax.axis_index("col")
    row = lax.axis_index("row")
    core = row % 2
    mate = row + 1 - 2 * core
    across = ((row // 2 + 1) % 2) * 2
    width, rows = feat_ref.shape
    ranks = left_ref.shape[0]
    chunks, _, cols = zpt.shape

    loads = [
        pltpu.make_async_copy(src, dst, l_sem.at[i])
        for i, (src, dst) in enumerate((
            (inv_hbm, inv_ref), (feat_hbm, feat_ref), (left_hbm, left_ref),
            (pts_hbm, pts_ref), (right_hbm, right_ref),
        ))
    ]
    for load in loads:
        load.start()

    def peer(d):
        out = 0
        bit = 1
        while bit < n:
            out = out + (((me // bit) % 2 + (d // bit) % 2) % 2) * bit
            bit *= 2
        return out

    barrier = pltpu.get_barrier_semaphore()
    for d in range(1, n):
        pl.semaphore_signal(barrier, inc=1, device_id={"col": peer(d)}, device_id_type=MESH)
    for r in (mate, across, across + 1):
        pl.semaphore_signal(barrier, inc=1, device_id={"row": r}, device_id_type=MESH)

    loads[0].wait()
    eye = lax.broadcasted_iota(jnp.int32, (width, width), 0) == lax.broadcasted_iota(
        jnp.int32, (width, width), 1
    )
    inv = jnp.sum(jnp.where(eye, inv_ref[...], 0.0), axis=1, keepdims=True)
    loads[1].wait()
    loads[2].wait()
    gin[0, :width, :] = (feat_ref[...].astype(F32) * inv).astype(BF16)
    rank = lax.broadcasted_iota(jnp.int32, (ranks, rows), 0)
    coef = jnp.where(rank == 0, jnp.float32(0.5), jnp.float32(-0.5 / (ranks - 1)))
    gin[0, width:, :] = (left_ref[...].astype(F32) * coef * (64.0 / math.sqrt(total))).astype(BF16)
    pl.semaphore_wait(barrier, n + 2)

    def gather(d):
        return pltpu.make_async_remote_copy(
            src_ref=gin.at[0], dst_ref=gin.at[d], send_sem=g_send.at[d], recv_sem=g_recv.at[d],
            device_id={"col": peer(d)}, device_id_type=MESH,
        )

    def forward(d):
        return pltpu.make_async_remote_copy(
            src_ref=gin.at[d], dst_ref=gin.at[d + 1], send_sem=f_send.at[d],
            recv_sem=g_recv.at[d + 1], device_id={"col": peer(1)}, device_id_type=MESH,
        )

    def giveback(d):
        return pltpu.make_async_remote_copy(
            src_ref=back_out.at[d], dst_ref=back_in.at[d], send_sem=r_send.at[d],
            recv_sem=r_recv.at[d], device_id={"col": peer(d)}, device_id_type=MESH,
        )

    def stage_a(h):
        return pltpu.make_async_remote_copy(
            src_ref=a_own.at[h], dst_ref=a_in.at[h], send_sem=a_send.at[h],
            recv_sem=a_recv.at[h], device_id={"row": mate}, device_id_type=MESH,
        )

    def stage_b(h, side, slot):
        return pltpu.make_async_remote_copy(
            src_ref=b_own.at[h, slot], dst_ref=b_in.at[h, slot], send_sem=b_send.at[h, side],
            recv_sem=b_recv.at[h, slot], device_id={"row": across + side}, device_id_type=MESH,
        )

    for d in range(2, n, 2):
        gather(d).start()
    gather(1).start()

    loads[3].wait()
    loads[4].wait()
    for h in range(chunks):
        part = pl.ds(h * cols, cols)
        zs = (pts_ref[:, part].astype(F32) * inv).astype(BF16).astype(F32)
        zt = jnp.concatenate(
            [zs, tail_rows(zs, ONE_X, ONE_Z), jnp.zeros((128 - LEFT, cols), F32)], axis=0
        )
        zpt[h] = zt.astype(BF16)
        zp[h] = zt.T.astype(BF16)
        rpt[h] = jnp.concatenate(
            [
                jnp.zeros((LEFT, cols), BF16),
                right_ref[:, part],
                jnp.zeros((128 - LEFT - ranks, cols), BF16),
            ],
            axis=0,
        )

    def send_a(h):
        zt = zpt[h, :width, :].astype(F32)
        term = tr[h, :width, :] - tr[h, ONE_X:ONE_X + 1, :] * zt
        a_own[h] = term.astype(BF16)
        stage_a(h).start()

    def send_b(h):
        stage_a(h).wait()
        s = (a_own[h].astype(F32) + a_in[h].astype(F32)).astype(BF16)
        b_own[h, 0] = s[:, : cols // 2]
        b_own[h, 1] = s[:, cols // 2:]
        for side in range(2):
            stage_b(h, side, core).start()

    def finish(h):
        for side in range(2):
            stage_b(h, side, core).wait_send()
        for slot in range(2):
            stage_b(h, 0, slot).wait_recv()
        tot = b_own[h].astype(F32) + b_in[h].astype(F32)
        part = pl.ds(h * cols, cols)
        point_ref[:, part] = jnp.concatenate([tot[0], tot[1]], axis=1) * inv

    def step(i, carry):
        early = i < 4
        late = i >= n + 2
        h = jnp.where(early, i % 2, jnp.where(late, 1, 0))
        k = i - 2
        even = k <= n // 2
        near = jnp.where(even, 2 * k - 2, 2 * k - n + 1)
        d = jnp.where(early, i // 2, jnp.where(late, 2 * n + 1 - i, near))
        last = h == 1

        @pl.when((h == 0) & (d > 0))
        def _():
            gather(d).wait_recv()

        @pl.when((h == 0) & (d > 1) & even)
        def _():
            forward(d).start()

        @pl.when(h == 0)
        def _():
            x = gin[d].astype(F32)
            xs = x[:width]
            both = jnp.concatenate(
                [
                    xs, tail_rows(xs, ONE_Z, ONE_X), x[width:],
                    jnp.zeros((128 - LEFT - ranks, rows), F32),
                ],
                axis=0,
            )
            pkt[d] = both[:LEFT].astype(BF16)
            pk[d] = both.T.astype(BF16)

        block = pk[d]
        arg = jnp.dot(block, zpt[h], preferred_element_type=F32)
        weight = jnp.dot(block, rpt[h], preferred_element_type=F32)
        prod = (weight * jnp.exp(arg)).astype(BF16)
        g = jnp.dot(prod, zp[h], preferred_element_type=F32)
        t = jnp.dot(pkt[d], prod, preferred_element_type=F32)
        gz[d] = jnp.where(h == 0, 0.0, gz[d]) + g
        tr[h] = jnp.where(d == 0, 0.0, tr[h]) + t

        @pl.when(last)
        def _():
            acc = gz[d].T
            term = acc[:width] - acc[ONE_Z:ONE_Z + 1] * pkt[d][:width].astype(F32)

            @pl.when(d > 0)
            def _():
                back_out[d] = term.astype(BF16)
                giveback(d).start()

            @pl.when(d == 0)
            def _():
                slab_ref[...] = term

        @pl.when(i == n + 1)
        def _():
            send_a(0)

        @pl.when(i == n + 3)
        def _():
            send_b(0)

        @pl.when(i == 2 * n - 1)
        def _():
            send_a(1)
            finish(0)

        return carry

    lax.fori_loop(0, 2 * n, step, 0)

    gather(1).wait_send()
    for d in range(2, n, 2):
        gather(d).wait_send()
        forward(d).wait_send()
    send_b(1)
    for d in range(1, n):
        giveback(d).wait()

    def add(d, acc):
        return acc + back_in[d].astype(F32)

    slab_ref[...] = lax.fori_loop(1, n, add, slab_ref[...]) * inv
    finish(1)


def local(n, slab_feat, slab_left, points, right_vec, inv_length):
    rows, width = slab_feat.shape
    ranks = slab_left.shape[1]
    npts = points.shape[0]
    cols = npts // CHUNKS
    vm = pl.BlockSpec(memory_space=pltpu.VMEM)
    hbm = pl.BlockSpec(memory_space=pltpu.HBM)
    dma = pltpu.SemaphoreType.DMA
    flops = 2 * n * rows * npts * 4 * 128
    operands = (slab_feat.T, slab_left.T, points.T, right_vec.T, inv_length.reshape(1, width))
    slab, point = pl.pallas_call(
        functools.partial(kernel, n, npts * n),
        out_shape=(
            jax.ShapeDtypeStruct((width, rows), F32),
            jax.ShapeDtypeStruct((width, npts), F32),
        ),
        in_specs=[hbm] * 5,
        out_specs=(vm, vm),
        scratch_shapes=[
            pltpu.VMEM((width, rows), BF16),
            pltpu.VMEM((ranks, rows), BF16),
            pltpu.VMEM((width, npts), BF16),
            pltpu.VMEM((ranks, npts), BF16),
            pltpu.VMEM((1, width), F32),
            pltpu.VMEM((n, width + ranks, rows), BF16),
            pltpu.VMEM((n, rows, 128), BF16),
            pltpu.VMEM((n, LEFT, rows), BF16),
            pltpu.VMEM((CHUNKS, cols, 128), BF16),
            pltpu.VMEM((CHUNKS, 128, cols), BF16),
            pltpu.VMEM((CHUNKS, 128, cols), BF16),
            pltpu.VMEM((n, rows, 128), F32),
            pltpu.VMEM((CHUNKS, LEFT, cols), F32),
            pltpu.VMEM((n, width, rows), BF16),
            pltpu.VMEM((n, width, rows), BF16),
            pltpu.VMEM((CHUNKS, width, cols), BF16),
            pltpu.VMEM((CHUNKS, width, cols), BF16),
            pltpu.VMEM((CHUNKS, 2, width, cols // 2), BF16),
            pltpu.VMEM((CHUNKS, 2, width, cols // 2), BF16),
            dma((5,)),
            dma((n,)),
            dma((n,)),
            dma((n,)),
            dma((n,)),
            dma((n,)),
            dma((CHUNKS,)),
            dma((CHUNKS,)),
            dma((CHUNKS, 2)),
            dma((CHUNKS, 2)),
        ],
        compiler_params=pltpu.CompilerParams(
            collective_id=0, has_side_effects=True, vmem_limit_bytes=48 * 1024 * 1024
        ),
        cost_estimate=pl.CostEstimate(
            flops=flops, bytes_accessed=4 * 1024 * 1024, transcendentals=n * rows * npts
        ),
    )(*[pltpu.with_memory_space_constraint(v, pltpu.HBM) for v in operands])
    return slab.T, point.T


def solution(mesh):
    placed = (P(("row", "col"), None), P(("row", "col"), None), P("col", None), P("col", None), P())
    return jax.shard_map(
        functools.partial(local, mesh.shape["col"]),
        mesh=mesh,
        in_specs=placed,
        out_specs=(P(("row", "col"), None), P("col", None)),
        check_vma=False,
    )
```

```python
import functools
import math

import jax
import jax.numpy as jnp
from jax import lax
from jax.experimental import pallas as pl
from jax.experimental.pallas import tpu as pltpu
from jax.sharding import PartitionSpec as P

F32 = jnp.float32
BF16 = jnp.bfloat16
MESH = pl.DeviceIdType.MESH
CHUNKS = 2
ONE_X = 64
ONE_Z = 67
LEFT = 80


def split3(v):
    a = v.astype(BF16).astype(F32)
    b = (v - a).astype(BF16).astype(F32)
    return a, b, v - a - b


def tail_rows(scaled, first_sq, first_one):
    a, b, c = split3(-0.5 * jnp.sum(scaled * scaled, axis=0, keepdims=True))
    line = lax.broadcasted_iota(jnp.int32, (16, scaled.shape[1]), 0) + 64
    out = jnp.where((line >= first_one) & (line < first_one + 3), 1.0, 0.0)
    out = jnp.where(line == first_sq, a, out)
    out = jnp.where(line == first_sq + 1, b, out)
    return jnp.where(line == first_sq + 2, c, out)


def kernel(
    n, total, feat_hbm, left_hbm, pts_hbm, right_hbm, inv_hbm, slab_ref, point_ref,
    feat_ref, left_ref, pts_ref, right_ref, inv_ref,
    gin, pk, pkt, zp, zpt, rpt, gz, tr, back_out, back_in, a_own, a_in, b_own, b_in,
    l_sem, g_send, g_recv, f_send, r_send, r_recv, a_send, a_recv, b_send, b_recv,
):
    me = lax.axis_index("col")
    row = lax.axis_index("row")
    core = row % 2
    mate = row + 1 - 2 * core
    across = ((row // 2 + 1) % 2) * 2
    width, rows = feat_ref.shape
    ranks = left_ref.shape[0]
    chunks, _, cols = zpt.shape

    loads = [
        pltpu.make_async_copy(src, dst, l_sem.at[i])
        for i, (src, dst) in enumerate((
            (inv_hbm, inv_ref), (feat_hbm, feat_ref), (left_hbm, left_ref),
            (pts_hbm, pts_ref), (right_hbm, right_ref),
        ))
    ]
    for load in loads:
        load.start()

    def peer(d):
        out = 0
        bit = 1
        while bit < n:
            out = out + (((me // bit) % 2 + (d // bit) % 2) % 2) * bit
            bit *= 2
        return out

    barrier = pltpu.get_barrier_semaphore()
    for d in range(1, n):
        pl.semaphore_signal(barrier, inc=1, device_id={"col": peer(d)}, device_id_type=MESH)
    for r in (mate, across, across + 1):
        pl.semaphore_signal(barrier, inc=1, device_id={"row": r}, device_id_type=MESH)

    loads[0].wait()
    eye = lax.broadcasted_iota(jnp.int32, (width, width), 0) == lax.broadcasted_iota(
        jnp.int32, (width, width), 1
    )
    inv = jnp.sum(jnp.where(eye, inv_ref[...], 0.0), axis=1, keepdims=True)
    loads[1].wait()
    loads[2].wait()
    gin[0, :width, :] = (feat_ref[...].astype(F32) * inv).astype(BF16)
    rank = lax.broadcasted_iota(jnp.int32, (ranks, rows), 0)
    coef = jnp.where(rank == 0, jnp.float32(0.5), jnp.float32(-0.5 / (ranks - 1)))
    gin[0, width:, :] = (left_ref[...].astype(F32) * coef * (64.0 / math.sqrt(total))).astype(BF16)
    pl.semaphore_wait(barrier, n + 2)

    def gather(d):
        return pltpu.make_async_remote_copy(
            src_ref=gin.at[0], dst_ref=gin.at[d], send_sem=g_send.at[d], recv_sem=g_recv.at[d],
            device_id={"col": peer(d)}, device_id_type=MESH,
        )

    def forward(d):
        return pltpu.make_async_remote_copy(
            src_ref=gin.at[d], dst_ref=gin.at[d + 1], send_sem=f_send.at[d],
            recv_sem=g_recv.at[d + 1], device_id={"col": peer(1)}, device_id_type=MESH,
        )

    def giveback(d):
        return pltpu.make_async_remote_copy(
            src_ref=back_out.at[d], dst_ref=back_in.at[d], send_sem=r_send.at[d],
            recv_sem=r_recv.at[d], device_id={"col": peer(d)}, device_id_type=MESH,
        )

    def stage_a(h):
        return pltpu.make_async_remote_copy(
            src_ref=a_own.at[h], dst_ref=a_in.at[h], send_sem=a_send.at[h],
            recv_sem=a_recv.at[h], device_id={"row": mate}, device_id_type=MESH,
        )

    def stage_b(h, side, slot):
        return pltpu.make_async_remote_copy(
            src_ref=b_own.at[h, slot], dst_ref=b_in.at[h, slot], send_sem=b_send.at[h, side],
            recv_sem=b_recv.at[h, slot], device_id={"row": across + side}, device_id_type=MESH,
        )

    for d in range(2, n, 2):
        gather(d).start()
    gather(1).start()

    loads[3].wait()
    loads[4].wait()
    for h in range(chunks):
        part = pl.ds(h * cols, cols)
        zs = (pts_ref[:, part].astype(F32) * inv).astype(BF16).astype(F32)
        zt = jnp.concatenate(
            [zs, tail_rows(zs, ONE_X, ONE_Z), jnp.zeros((128 - LEFT, cols), F32)], axis=0
        )
        zpt[h] = zt.astype(BF16)
        zp[h] = zt.T.astype(BF16)
        rpt[h] = jnp.concatenate(
            [
                jnp.zeros((LEFT, cols), BF16),
                right_ref[:, part],
                jnp.zeros((128 - LEFT - ranks, cols), BF16),
            ],
            axis=0,
        )

    def send_a(h):
        zt = zpt[h, :width, :].astype(F32)
        term = tr[h, :width, :] - tr[h, ONE_X:ONE_X + 1, :] * zt
        a_own[h] = term.astype(BF16)
        stage_a(h).start()

    def send_b(h):
        stage_a(h).wait()
        s = (a_own[h].astype(F32) + a_in[h].astype(F32)).astype(BF16)
        b_own[h, 0] = s[:, : cols // 2]
        b_own[h, 1] = s[:, cols // 2:]
        for side in range(2):
            stage_b(h, side, core).start()

    def finish(h):
        for side in range(2):
            stage_b(h, side, core).wait_send()
        for slot in range(2):
            stage_b(h, 0, slot).wait_recv()
        tot = b_own[h].astype(F32) + b_in[h].astype(F32)
        part = pl.ds(h * cols, cols)
        point_ref[:, part] = jnp.concatenate([tot[0], tot[1]], axis=1) * inv

    def step(i, carry):
        early = i < 4
        late = i >= n + 2
        h = jnp.where(early, i % 2, jnp.where(late, 1, 0))
        k = i - 2
        even = k <= n // 2
        near = jnp.where(even, 2 * k - 2, 2 * k - n + 1)
        d = jnp.where(early, i // 2, jnp.where(late, 2 * n + 1 - i, near))
        last = h == 1

        @pl.when((h == 0) & (d % 2 == 1))
        def _():
            gather(d).wait_recv()

        @pl.when((i >= 3) & (i < n // 2 + 2))
        def _():
            gather(2 * (i - 2)).wait_recv()
            forward(2 * (i - 2)).start()

        @pl.when(h == 0)
        def _():
            x = gin[d].astype(F32)
            xs = x[:width]
            both = jnp.concatenate(
                [
                    xs, tail_rows(xs, ONE_Z, ONE_X), x[width:],
                    jnp.zeros((128 - LEFT - ranks, rows), F32),
                ],
                axis=0,
            )
            pkt[d] = both[:LEFT].astype(BF16)
            pk[d] = both.T.astype(BF16)

        block = pk[d]
        arg = jnp.dot(block, zpt[h], preferred_element_type=F32)
        weight = jnp.dot(block, rpt[h], preferred_element_type=F32)
        prod = (weight * jnp.exp(arg)).astype(BF16)
        g = jnp.dot(prod, zp[h], preferred_element_type=F32)
        t = jnp.dot(pkt[d], prod, preferred_element_type=F32)
        gz[d] = jnp.where(h == 0, 0.0, gz[d]) + g
        tr[h] = jnp.where(d == 0, 0.0, tr[h]) + t

        @pl.when(last)
        def _():
            acc = gz[d].T
            term = acc[:width] - acc[ONE_Z:ONE_Z + 1] * pkt[d][:width].astype(F32)

            @pl.when(d > 0)
            def _():
                back_out[d] = term.astype(BF16)
                giveback(d).start()

            @pl.when(d == 0)
            def _():
                slab_ref[...] = term

        @pl.when(i == n + 1)
        def _():
            send_a(0)

        @pl.when(i == n + 3)
        def _():
            send_b(0)

        @pl.when(i == 2 * n - 1)
        def _():
            send_a(1)
            finish(0)

        return carry

    lax.fori_loop(0, 2 * n, step, 0)

    gather(1).wait_send()
    for d in range(2, n, 2):
        gather(d).wait_send()
        forward(d).wait_send()
    send_b(1)
    for d in range(1, n):
        giveback(d).wait()

    def add(d, acc):
        return acc + back_in[d].astype(F32)

    slab_ref[...] = lax.fori_loop(1, n, add, slab_ref[...]) * inv
    finish(1)


def local(n, slab_feat, slab_left, points, right_vec, inv_length):
    rows, width = slab_feat.shape
    ranks = slab_left.shape[1]
    npts = points.shape[0]
    cols = npts // CHUNKS
    vm = pl.BlockSpec(memory_space=pltpu.VMEM)
    hbm = pl.BlockSpec(memory_space=pltpu.HBM)
    dma = pltpu.SemaphoreType.DMA
    flops = 2 * n * rows * npts * 4 * 128
    operands = (slab_feat.T, slab_left.T, points.T, right_vec.T, inv_length.reshape(1, width))
    slab, point = pl.pallas_call(
        functools.partial(kernel, n, npts * n),
        out_shape=(
            jax.ShapeDtypeStruct((width, rows), F32),
            jax.ShapeDtypeStruct((width, npts), F32),
        ),
        in_specs=[hbm] * 5,
        out_specs=(vm, vm),
        scratch_shapes=[
            pltpu.VMEM((width, rows), BF16),
            pltpu.VMEM((ranks, rows), BF16),
            pltpu.VMEM((width, npts), BF16),
            pltpu.VMEM((ranks, npts), BF16),
            pltpu.VMEM((1, width), F32),
            pltpu.VMEM((n, width + ranks, rows), BF16),
            pltpu.VMEM((n, rows, 128), BF16),
            pltpu.VMEM((n, LEFT, rows), BF16),
            pltpu.VMEM((CHUNKS, cols, 128), BF16),
            pltpu.VMEM((CHUNKS, 128, cols), BF16),
            pltpu.VMEM((CHUNKS, 128, cols), BF16),
            pltpu.VMEM((n, rows, 128), F32),
            pltpu.VMEM((CHUNKS, LEFT, cols), F32),
            pltpu.VMEM((n, width, rows), BF16),
            pltpu.VMEM((n, width, rows), BF16),
            pltpu.VMEM((CHUNKS, width, cols), BF16),
            pltpu.VMEM((CHUNKS, width, cols), BF16),
            pltpu.VMEM((CHUNKS, 2, width, cols // 2), BF16),
            pltpu.VMEM((CHUNKS, 2, width, cols // 2), BF16),
            dma((5,)),
            dma((n,)),
            dma((n,)),
            dma((n,)),
            dma((n,)),
            dma((n,)),
            dma((CHUNKS,)),
            dma((CHUNKS,)),
            dma((CHUNKS, 2)),
            dma((CHUNKS, 2)),
        ],
        compiler_params=pltpu.CompilerParams(
            collective_id=0, has_side_effects=True, vmem_limit_bytes=48 * 1024 * 1024
        ),
        cost_estimate=pl.CostEstimate(
            flops=flops, bytes_accessed=4 * 1024 * 1024, transcendentals=n * rows * npts
        ),
    )(*[pltpu.with_memory_space_constraint(v, pltpu.HBM) for v in operands])
    return slab.T, point.T


def solution(mesh):
    placed = (P(("row", "col"), None), P(("row", "col"), None), P("col", None), P("col", None), P())
    return jax.shard_map(
        functools.partial(local, mesh.shape["col"]),
        mesh=mesh,
        in_specs=placed,
        out_specs=(P(("row", "col"), None), P("col", None)),
        check_vma=False,
    )
```
